512 devices in a mesh: row: 16 (over z), col: 32 (over y, x, core).
Axes of the slice: x: 4, y: 4, z: 16, core: 2. Of those that a mesh axis runs over, the one named last changes fastest.
Arguments:
- centroids: float32 [3, 32768], P(None, ('col', 'row')), may hold values from 0 to 1, as said below
- areas: float32 [32768], P(('col', 'row')), may hold values from 0.5 to 2
- conductance: float32 [32768], P(('col', 'row')), may hold values from 0.1 to 1
- power: float32 [16, 32768], P(None, ('col', 'row')), may hold values from -3 to 6
Outputs:
- solution: float32 [16, 32768], P(None, ('col', 'row'))
- residual: float32 [16, 32768], P(None, ('col', 'row'))
The draws below stay inside these ranges and needn't reach their ends.
Inputs may be any that keep to these rules, and one draw needn't show every extreme that they name: `centroids`: panels lie on 16 parallel fins across the unit cube.
All inputs are finite; a program needn't handle non-finite values.
Results may differ from the reference program's by a relative error of at most 0.00039.
Values may be sent and summed in bfloat16 or wider, within the bound.
No kernel may reach another device: no remote copies, remote signals or barrier semaphores. Data moves between devices by JAX's collectives and lax.ppermute only.
A program may use at most 64 MiB of HBM per device.

```python
import math
import jax
import jax.numpy as jnp
from jax import lax

RHS = 16
PANELS = 32768


def geometry(key):
    base = jax.random.fold_in(key, 11)
    key_fin, key_jit, key_face = jax.random.split(base, 3)
    fins = jax.random.randint(key_fin, (PANELS,), 0, 16)
    jitter = jax.random.uniform(key_jit, (PANELS,), jnp.float32, -0.01, 0.01)
    across = (fins.astype(jnp.float32) + 0.5) / 16.0 + jitter
    face = jax.random.uniform(key_face, (2, PANELS), jnp.float32, 0.0, 1.0)
    return jnp.stack([across, face[0], face[1]], 0)


def draw_centroids(key, part):
    return geometry(key)


def draw_power(key, part):
    points = geometry(key)
    base = jax.random.fold_in(key, 23)
    key_freq, key_phase, key_rough = jax.random.split(base, 3)
    freq = jax.random.uniform(key_freq, (RHS, 3), jnp.float32, 1.0, 4.0)
    phase = jax.random.uniform(key_phase, (RHS, 1), jnp.float32, -math.pi, math.pi)
    wave = freq[:, 0:1] * points[0][None, :] + freq[:, 1:2] * points[1][None, :] + freq[:, 2:3] * points[2][None, :]
    smooth = 0.5 * jnp.cos(2.0 * math.pi * wave + phase)
    rough = jnp.clip(jax.random.normal(key_rough, (RHS, PANELS), jnp.float32), -3.0, 3.0)
    return 1.0 + smooth + rough


def levels(stream_key, shape, cuts, smallest, largest):
    def one(dim, shards_of):
        steps = jax.random.uniform(jax.random.fold_in(jax.random.fold_in(stream_key, 6), dim), (shards_of,), jnp.float32, smallest / len(cuts), largest / len(cuts))
        return jnp.repeat(jnp.exp(steps), shape[dim] // shards_of).reshape((-1,) + (1,) * (len(shape) - dim - 1))

    factor_of = one(*cuts[0])
    for cut in cuts[1:]:
        factor_of = factor_of * one(*cut)
    return factor_of


def setup_inputs(seed: int = 0) -> dict:
    splits = jax.random.split(jax.random.key(seed), 5)
    centroids = draw_centroids(jax.random.fold_in(splits[4], 71), 0)
    areas = jnp.clip(jnp.exp(math.log(2.0) - 1.3862944 * jax.random.uniform(splits[1], (PANELS,), jnp.float32) ** levels(splits[1], (PANELS,), ((0, 512),), -0.2, 0.2)), 0.5, 2.0)
    conductance = jnp.clip(jnp.exp(math.log(1.0) - 2.3025851 * jax.random.uniform(splits[2], (PANELS,), jnp.float32) ** levels(splits[2], (PANELS,), ((0, 512),), -0.2, 0.2)), 0.1, 1.0)
    power = draw_power(jax.random.fold_in(splits[4], 71), 0)
    return dict(centroids=centroids, areas=areas, conductance=conductance, power=power)


def kernel_tile(src, tgt, scale, delta2):
    dx = src[0][:, None] - tgt[0][None, :]
    dy = src[1][:, None] - tgt[1][None, :]
    dz = src[2][:, None] - tgt[2][None, :]
    dist2 = dx * dx + dy * dy + dz * dz
    return (src[3][:, None] * scale * lax.rsqrt(dist2 + delta2)).astype(jnp.bfloat16)

def inner(left, right):
    return jnp.dot(left, right.T, precision=lax.Precision.HIGHEST)

def lower_inverse(gram):
    factor = jnp.linalg.cholesky(gram)
    eye = jnp.eye(gram.shape[0], dtype=jnp.float32)
    return (factor, jax.scipy.linalg.solve_triangular(factor, eye, lower=True))

def reference(centroids, areas, conductance, power):
    scale = 4.0 / (math.pi * PANELS)
    delta2 = 16.0 / PANELS
    sources = jnp.concatenate([centroids, areas[None, :]], 0)
    block = math.gcd(PANELS, 512)
    count = PANELS // block
    high = lax.Precision.HIGHEST

    def apply(field):
        rounded = lax.optimization_barrier(field.astype(jnp.bfloat16)).astype(jnp.float32)

        def one(index):
            tgt = lax.dynamic_slice_in_dim(centroids, index * block, block, 1)
            tile = lax.optimization_barrier(kernel_tile(sources, tgt, scale, delta2)).astype(jnp.float32)
            return jnp.dot(rounded, tile, precision=high)
        pieces = lax.map(one, jnp.arange(count, dtype=jnp.int32))
        product = pieces.transpose(1, 0, 2).reshape(RHS, PANELS)
        return conductance[None, :] * field + product
    factor0, inverse0 = lower_inverse(inner(power, power))
    basis = [jnp.dot(inverse0, power, precision=high)]
    blocks = {}
    for step in range(2):
        image = apply(basis[step])
        coeffs = [inner(vec, image) for vec in basis]
        for idx in range(step + 1):
            image = image - jnp.dot(coeffs[idx].T, basis[idx], precision=high)
            blocks[idx, step] = coeffs[idx]
        factor, inverse = lower_inverse(inner(image, image))
        blocks[step + 1, step] = factor.T
        basis.append(jnp.dot(inverse, image, precision=high))
    hbar = jnp.zeros((3 * RHS, 2 * RHS), jnp.float32)
    for key in blocks:
        hbar = hbar.at[key[0] * RHS:(key[0] + 1) * RHS, key[1] * RHS:(key[1] + 1) * RHS].set(blocks[key])
    target = jnp.zeros((3 * RHS, RHS), jnp.float32).at[:RHS].set(factor0.T)
    normal = jnp.dot(hbar.T, hbar, precision=high)
    chol = jnp.linalg.cholesky(normal)
    coeff_y = jax.scipy.linalg.cho_solve((chol, True), jnp.dot(hbar.T, target, precision=high))
    coeff_z = target - jnp.dot(hbar, coeff_y, precision=high)
    solution = jnp.dot(coeff_y[:RHS].T, basis[0], precision=high) + jnp.dot(coeff_y[RHS:].T, basis[1], precision=high)
    residual = jnp.dot(coeff_z[:RHS].T, basis[0], precision=high) + jnp.dot(coeff_z[RHS:2 * RHS].T, basis[1], precision=high)
    residual = residual + jnp.dot(coeff_z[2 * RHS:].T, basis[2], precision=high)
    return (solution, residual)
```

```python
import math

import jax
import jax.numpy as jnp
from jax import lax
from jax.sharding import PartitionSpec as P

HIGH = lax.Precision.HIGHEST


def kernel_tile(src, tgt, scale, delta2):
    dx = src[0][:, None] - tgt[0][None, :]
    dy = src[1][:, None] - tgt[1][None, :]
    dz = src[2][:, None] - tgt[2][None, :]
    dist2 = dx * dx + dy * dy + dz * dz
    return (src[3][:, None] * scale * lax.rsqrt(dist2 + delta2)).astype(jnp.bfloat16)


def inner(left, right):
    return jnp.dot(left, right.T, precision=HIGH)


def lower_inverse(gram):
    factor = jnp.linalg.cholesky(gram)
    eye = jnp.eye(gram.shape[0], dtype=jnp.float32)
    return jax.scipy.linalg.solve_triangular(factor, eye, lower=True)


def spread(chunk, axis):
    size = lax.axis_size(axis)
    return lax.all_to_all(jnp.broadcast_to(chunk[None], (size,) + chunk.shape), axis, 0, 0)


def wide(parts):
    return parts.transpose(1, 0, 2).reshape(parts.shape[1], -1)


def body(centroids, areas, conductance, power):
    nrhs, width = power.shape
    rows, cols = lax.axis_size("row"), lax.axis_size("col")
    panels = width * rows * cols
    scale = 4.0 / (math.pi * panels)
    delta2 = 16.0 / panels
    cond_row = conductance[None, :]
    near = spread(jnp.concatenate([power, centroids, areas[None, :], cond_row], 0), "row")
    near = wide(near)
    power_near, sources = near[:nrhs], near[nrhs : nrhs + 4]
    gram0 = inner(power_near, power_near)
    mean = jnp.sum(near[nrhs + 4]) / panels
    pack = jnp.concatenate(
        [centroids.reshape(-1), gram0.reshape(-1), jnp.full((64,), mean)], 0
    ).reshape(-1, 128)
    far = spread(pack, "col").reshape(cols, -1)
    targets = wide(far[:, : 3 * width].reshape(cols, 3, width))
    total = jnp.sum(far[:, 3 * width :], 0)
    theta = total[nrhs * nrhs]
    inverse0 = lower_inverse(total[: nrhs * nrhs].reshape(nrhs, nrhs))
    v_near = jnp.dot(inverse0, power_near, precision=HIGH)
    v_own = jnp.dot(inverse0, power, precision=HIGH)
    tile = kernel_tile(sources, targets, scale, delta2)

    def scatter(partial):
        parts = partial.reshape(nrhs, cols, width).transpose(1, 0, 2)
        return jnp.sum(lax.all_to_all(parts, "col", 0, 0), 0)

    product = scatter(
        jnp.dot(v_near.astype(jnp.bfloat16), tile, preferred_element_type=jnp.float32)
    )
    w1 = cond_row * v_own + product
    u_near = wide(spread(w1, "row")) - theta * v_near
    u_own = w1 - theta * v_own
    high = u_near.astype(jnp.bfloat16)
    low = (u_near - high.astype(jnp.float32)).astype(jnp.bfloat16)
    both = jnp.dot(jnp.concatenate([high, low], 0), tile, preferred_element_type=jnp.float32)
    w2 = cond_row * u_own + scatter(both[:nrhs] + both[nrhs:])
    stack = jnp.concatenate([w1, w2, power], 0)
    gram = inner(stack[: 2 * nrhs], stack).reshape(-1, 128)
    gram = jnp.sum(spread(gram, "col"), 0)
    gram = jnp.sum(spread(gram, "row"), 0).reshape(2 * nrhs, 3 * nrhs)
    inverse = lower_inverse(gram[:, : 2 * nrhs])
    coeff = jnp.dot(
        inverse.T, jnp.dot(inverse, gram[:, 2 * nrhs :], precision=HIGH), precision=HIGH
    )
    basis = jnp.concatenate([v_own, u_own], 0)
    solution = jnp.dot(coeff.T, basis, precision=HIGH)
    residual = power - jnp.dot(coeff.T, stack[: 2 * nrhs], precision=HIGH)
    return (solution, residual)


def solution(mesh):
    return jax.shard_map(
        body,
        mesh=mesh,
        in_specs=(
            P(None, ("col", "row")),
            P(("col", "row")),
            P(("col", "row")),
            P(None, ("col", "row")),
        ),
        out_specs=(P(None, ("col", "row")), P(None, ("col", "row"))),
        check_vma=False,
    )
```

```python
import functools
import math

import jax
import jax.numpy as jnp
from jax import lax
from jax.experimental import pallas as pl
from jax.experimental.pallas import tpu as pltpu
from jax.sharding import PartitionSpec as P

HIGH = lax.Precision.HIGHEST
F32 = jnp.float32
BF16 = jnp.bfloat16


def mm(a, b):
    return jnp.dot(a, b, precision=HIGH, preferred_element_type=F32)


def mm_t(a, b):
    return lax.dot_general(
        a, b, (((1,), (1,)), ((), ())), precision=HIGH, preferred_element_type=F32
    )


def t_mm(a, b):
    return lax.dot_general(
        a, b, (((0,), (0,)), ((), ())), precision=HIGH, preferred_element_type=F32
    )


def call(fn, outs, *args, scratch=()):
    vmem = pl.BlockSpec(memory_space=pltpu.VMEM)
    return pl.pallas_call(
        fn,
        out_shape=tuple(jax.ShapeDtypeStruct(shape, dtype) for shape, dtype in outs),
        in_specs=[vmem] * len(args),
        out_specs=tuple(vmem for _ in outs),
        scratch_shapes=list(scratch),
        compiler_params=pltpu.CompilerParams(vmem_limit_bytes=32 * 1024 * 1024),
    )(*args)


def forward(gram, right):
    n = gram.shape[0]
    a = jnp.concatenate([gram, right], 1)
    row_id = lax.broadcasted_iota(jnp.int32, (n, 1), 0)
    scale = jnp.zeros((n, 1), F32)
    for k in range(n):
        pivot = a[k : k + 1, k : k + 1]
        col = a[:, k : k + 1] * (1.0 / pivot)
        scale = jnp.where(row_id == k, lax.rsqrt(pivot), scale)
        a = a - jnp.where(row_id > k, col, 0.0) * a[k : k + 1, :]
    return a[:, n:] * scale


def identity(n):
    return (
        lax.broadcasted_iota(jnp.int32, (n, n), 0) == lax.broadcasted_iota(jnp.int32, (n, n), 1)
    ).astype(F32)


def solve(gram, right):
    n = gram.shape[0]
    a = jnp.concatenate([gram, right], 1)
    row_id = lax.broadcasted_iota(jnp.int32, (n, 1), 0)
    for k in range(n):
        inv = 1.0 / a[k : k + 1, k : k + 1]
        pivot_row = a[k : k + 1, :] * inv
        col = jnp.where(row_id == k, 0.0, a[:, k : k + 1])
        a = jnp.where(row_id == k, pivot_row, a - col * pivot_row)
    return a[:, n:]


def spread_out(ref, chunk):
    for i in range(ref.shape[0]):
        ref[i] = chunk


def tree_sum(ref):
    parts = [ref[i] for i in range(ref.shape[0])]
    while len(parts) > 1:
        parts = [parts[i] + parts[i + 1] for i in range(0, len(parts), 2)]
    return parts[0]


def left_pairs(ref, rows):
    return jnp.concatenate([ref[i, rows, :64] for i in range(ref.shape[0])], 1)


def pack_kernel(cen, area, cond, power, out, tmp):
    tmp[...] = jnp.zeros_like(tmp)
    tmp[:, :64] = power[...]
    tmp[0:3, 64:] = cen[...]
    tmp[3:4, 64:] = area[...]
    tmp[4:5, 64:] = cond[...]
    spread_out(out, tmp[...])


def near_kernel(scale, near, cen, out, power_near, src, tmp):
    p = jnp.concatenate([near[i, :, :64] for i in range(near.shape[0])], 1)
    g = jnp.concatenate([near[i, 0:8, 64:] for i in range(near.shape[0])], 1)
    power_near[...] = p
    row_id = lax.broadcasted_iota(jnp.int32, g.shape, 0)
    src[...] = jnp.where(row_id == 3, g * scale, g)
    gram = mm_t(p, p)
    tmp[...] = jnp.zeros_like(tmp)
    tmp[0:3, :64] = cen[...]
    tmp[3:4, :64] = jnp.broadcast_to(jnp.sum(g[4:5, :], 1, keepdims=True), (1, 64))
    tmp[:, 64:80] = gram[:8]
    tmp[:, 80:96] = gram[8:]
    spread_out(out, tmp[...])


def first_kernel(panels, far, power_near, power, tgt, v_near, v_bf, v_own, theta):
    tgt[...] = jnp.concatenate([far[i, :, :64] for i in range(far.shape[0])], 1)
    total = tree_sum(far)
    gram = jnp.concatenate([total[:, 64:80], total[:, 80:96]], 0)
    theta[...] = jnp.broadcast_to(total[3:4, 0:1] * (1.0 / panels), theta.shape)
    inverse = forward(gram, identity(gram.shape[0]))
    v = mm(inverse, power_near[...])
    v_near[...] = v
    v_bf[...] = v.astype(BF16)
    v_own[...] = mm(inverse, power[...])


def second_kernel(recv, cond, v_own, theta, out, w_own, u_own, tmp):
    total = tree_sum(recv)
    product = jnp.concatenate([total[:, :64], total[:, 64:]], 0)
    w = cond[...] * v_own[...] + product
    u = w - theta[0:1, 0:64] * v_own[...]
    w_own[...] = w
    u_own[...] = u
    tmp[:, :64] = u
    tmp[:, 64:] = jnp.zeros_like(u)
    spread_out(out, tmp[...])


def third_kernel(recv, v_near, u_split, gram):
    u = jnp.concatenate([recv[i, :, :64] for i in range(recv.shape[0])], 1)
    high = u.astype(BF16)
    u_split[0:16] = high
    u_split[16:32] = (u - high.astype(F32)).astype(BF16)
    gram[...] = jnp.concatenate([mm_t(v_near[...], u), mm_t(u, u)], 1)


def fourth_kernel(partial, gram, out):
    both = partial[0:16] + partial[16:32]
    extra = jnp.concatenate([gram[...], jnp.zeros((16, 32), F32)], 1)
    for i in range(out.shape[0]):
        out[i, :, :64] = both[:, i * 64 : i * 64 + 64]
        out[i, :, 64:] = extra


def fifth_kernel(recv, cond, v_own, w_own, u_own, power, out, basis, images, tmp):
    total = tree_sum(recv)
    shifted = total[:, 64:80]
    gram = total[:, 80:96]
    v, w, u = v_own[...], w_own[...], u_own[...]
    x = cond[...] * u + total[:, :64]
    both = jnp.concatenate([x, u], 1) - t_mm(shifted, jnp.concatenate([w, v], 1))
    both = forward(gram - t_mm(shifted, shifted), both)
    images[0:16] = w
    images[16:32] = both[:, :64]
    basis[0:16] = v
    basis[16:32] = both[:, 64:]
    stack = jnp.concatenate([images[...], power[...]], 0)
    small = mm_t(images[...], stack)
    tmp[...] = jnp.zeros_like(tmp)
    tmp[:, 0:48] = small[:16]
    tmp[:, 64:112] = small[16:]
    spread_out(out, tmp[...])


def sixth_kernel(recv, out):
    spread_out(out, tree_sum(recv))


def last_kernel(recv, basis, images, power, sol, res):
    total = tree_sum(recv)
    system = jnp.concatenate([total[:, 0:48], total[:, 64:112]], 0)
    coeff = solve(system[:, :32], system[:, 32:])
    sol[...] = t_mm(coeff, basis[...])
    res[...] = power[...] - t_mm(coeff, images[...])


def kernel_tile(src, tgt, delta2):
    dx = src[0][:, None] - tgt[0][None, :]
    dy = src[1][:, None] - tgt[1][None, :]
    dz = src[2][:, None] - tgt[2][None, :]
    dist2 = dx * dx + dy * dy + dz * dz
    return (src[3][:, None] * lax.rsqrt(dist2 + delta2)).astype(BF16)


def exchange(parts, axis):
    return lax.all_to_all(parts, axis, 0, 0)


def body(centroids, areas, conductance, power):
    nrhs, width = power.shape
    rows, cols = lax.axis_size("row"), lax.axis_size("col")
    panels = width * rows * cols
    scale = 4.0 / (math.pi * panels)
    delta2 = 16.0 / panels
    area, cond = areas[None, :], conductance[None, :]
    n_near, n_far = width * rows, width * cols
    (chunk,) = call(
        pack_kernel, [((rows, 16, 128), F32)], centroids, area, cond, power,
        scratch=[pltpu.VMEM((16, 128), F32)],
    )
    near = exchange(chunk, "row")
    chunk, power_near, src = call(
        functools.partial(near_kernel, scale),
        [((cols, 8, 128), F32), ((16, n_near), F32), ((8, n_near), F32)],
        near, centroids,
        scratch=[pltpu.VMEM((8, 128), F32)],
    )
    far = exchange(chunk, "col")
    tgt, v_near, v_bf, v_own, theta = call(
        functools.partial(first_kernel, panels),
        [((8, n_far), F32), ((16, n_near), F32), ((16, n_near), BF16), ((16, width), F32), ((1, 128), F32)],
        far, power_near, power,
    )
    tile = kernel_tile(src, tgt, delta2)
    partial = jnp.dot(v_bf, tile, preferred_element_type=F32)
    parts = partial.reshape(2, 8, cols, width).transpose(2, 1, 0, 3).reshape(cols, 8, 128)
    recv = exchange(parts, "col")
    chunk, w_own, u_own = call(
        second_kernel, [((rows, 16, 128), F32), ((16, width), F32), ((16, width), F32)],
        recv, cond, v_own, theta,
        scratch=[pltpu.VMEM((16, 128), F32)],
    )
    recv = exchange(chunk, "row")
    u_split, gram = call(
        third_kernel, [((32, n_near), BF16), ((16, 32), F32)], recv, v_near
    )
    partial = jnp.dot(u_split, tile, preferred_element_type=F32)
    (parts,) = call(fourth_kernel, [((cols, 16, 128), F32)], partial, gram)
    recv = exchange(parts, "col")
    chunk, basis, images = call(
        fifth_kernel,
        [((cols, 16, 128), F32), ((32, width), F32), ((32, width), F32)],
        recv, cond, v_own, w_own, u_own, power,
        scratch=[pltpu.VMEM((16, 128), F32)],
    )
    recv = exchange(chunk, "col")
    (chunk,) = call(sixth_kernel, [((rows, 16, 128), F32)], recv)
    recv = exchange(chunk, "row")
    return call(
        last_kernel, [((16, width), F32), ((16, width), F32)], recv, basis, images, power
    )


def solution(mesh):
    return jax.shard_map(
        body,
        mesh=mesh,
        in_specs=(
            P(None, ("col", "row")),
            P(("col", "row")),
            P(("col", "row")),
            P(None, ("col", "row")),
        ),
        out_specs=(P(None, ("col", "row")), P(None, ("col", "row"))),
        check_vma=False,
    )
```

```python
import functools
import math

import jax
import jax.numpy as jnp
from jax import lax
from jax.experimental import pallas as pl
from jax.experimental.pallas import tpu as pltpu
from jax.sharding import PartitionSpec as P

HIGH = lax.Precision.HIGHEST
F32 = jnp.float32
BF16 = jnp.bfloat16


def mm(a, b):
    return jnp.dot(a, b, precision=HIGH, preferred_element_type=F32)


def mm_t(a, b):
    return lax.dot_general(
        a, b, (((1,), (1,)), ((), ())), precision=HIGH, preferred_element_type=F32
    )


def t_mm(a, b):
    return lax.dot_general(
        a, b, (((0,), (0,)), ((), ())), precision=HIGH, preferred_element_type=F32
    )


def call(fn, outs, *args, scratch=()):
    vmem = pl.BlockSpec(memory_space=pltpu.VMEM)
    return pl.pallas_call(
        fn,
        out_shape=tuple(jax.ShapeDtypeStruct(shape, dtype) for shape, dtype in outs),
        in_specs=[pl.BlockSpec(memory_space=pltpu.VMEM)] * len(args),
        out_specs=tuple(vmem for _ in outs),
        scratch_shapes=list(scratch),
        compiler_params=pltpu.CompilerParams(vmem_limit_bytes=16 * 1024 * 1024),
    )(*args)


def block_pivots(a, n, below):
    row_id = lax.broadcasted_iota(jnp.int32, (n, 1), 0)
    for k in range(0, n, 2):
        row0, row1 = a[k : k + 1, :], a[k + 1 : k + 2, :]
        col0, col1 = a[:, k : k + 1], a[:, k + 1 : k + 2]
        p, q, r = row0[:, k : k + 1], row0[:, k + 1 : k + 2], row1[:, k + 1 : k + 2]
        inv = 1.0 / p
        ratio = q * inv
        inv_s = 1.0 / (r - q * ratio)
        row1 = row1 - ratio * row0
        col1 = col1 - ratio * col0
        if below:
            root0, root1 = lax.rsqrt(p), lax.rsqrt(r - q * ratio)
            new = a - jnp.where(row_id > k + 1, col0 * inv, 0.0) * row0
            new = new - jnp.where(row_id > k + 1, col1 * inv_s, 0.0) * row1
            a = jnp.where(row_id == k, row0 * root0, jnp.where(row_id == k + 1, row1 * root1, new))
        else:
            last = row1 * inv_s
            first = row0 * inv - ratio * last
            new = a - col0 * inv * row0 - col1 * last
            a = jnp.where(row_id == k, first, jnp.where(row_id == k + 1, last, new))
    return a[:, n:]


def forward(gram, right):
    return block_pivots(jnp.concatenate([gram, right], 1), gram.shape[0], True)


def identity(n):
    return (
        lax.broadcasted_iota(jnp.int32, (n, n), 0) == lax.broadcasted_iota(jnp.int32, (n, n), 1)
    ).astype(F32)


def solve(gram, right):
    return block_pivots(jnp.concatenate([gram, right], 1), gram.shape[0], False)


def spread_out(ref, chunk):
    for i in range(ref.shape[0]):
        ref[i] = chunk


def tree_sum(ref):
    parts = [ref[i] for i in range(ref.shape[0])]
    while len(parts) > 1:
        parts = [parts[i] + parts[i + 1] for i in range(0, len(parts), 2)]
    return parts[0]


def halves(ref, rows, side):
    lanes = slice(64 * side, 64 * side + 64)
    return jnp.concatenate([ref[i, rows, lanes] for i in range(ref.shape[0])], 1)


def split3(x):
    first = x.astype(BF16).astype(F32)
    second = (x - first).astype(BF16).astype(F32)
    return first, second, (x - first - second).astype(BF16).astype(F32)


def features(lefts, rights):
    out = [[], []]
    for left, right in zip(lefts, rights):
        for i, a in enumerate(left):
            for j, b in enumerate(right):
                if i + j < 3:
                    out[0].append(a)
                    out[1].append(b)
    n = len(out[0])
    for side in out:
        side.extend([jnp.zeros_like(side[0])] * (32 - n))
    return [jnp.concatenate(side, 0) for side in out]


def relay_kernel(block, twin, out):
    for i in range(out.shape[0]):
        out[i, 0:16] = block[...]
        out[i, 16:32] = twin[...]


def is_odd():
    return lax.rem(lax.axis_index("col"), 2) == 1


def swap_kernel(recv, out):
    odd = is_odd()
    for i in range(out.shape[0]):
        out[i, 0:8] = jnp.where(odd, recv[i, 0:8], recv[i, 16:24])
        out[i, 8:16] = jnp.where(odd, recv[i, 16:24], recv[i, 24:32])


def first_kernel(scale, delta2, recv, got, out, tile, power_near, left, right, split):
    odd = is_odd()
    count = recv.shape[0]
    near = [jnp.where(odd, got[i], recv[i, 0:16]) for i in range(count)]
    p = jnp.concatenate([x[:, :64] for x in near], 1)
    src = jnp.concatenate([x[0:8, 64:] for x in near], 1)
    far = []
    for i in range(count):
        far.append(jnp.where(odd, recv[i, 16:24], got[i, 8:16])[:, 64:])
        far.append(jnp.where(odd, recv[i, 0:8], got[i, 0:8])[:, 64:])
    t = jnp.concatenate(far, 1)[0:3] - 0.5
    power_near[...] = p
    high = p.astype(BF16)
    split[0:16] = high
    split[16:32] = (p - high.astype(F32)).astype(BF16)
    mean = jnp.broadcast_to(jnp.sum(src[4:5, :], 1, keepdims=True), (16, 16))
    extra = jnp.concatenate([mm_t(p, p), mean, jnp.zeros((16, 32), F32)], 1)
    s = src[0:3, :] - 0.5
    inv = 1.0 / (src[3:4, :] * scale)
    weight = inv * inv
    square = jnp.sum(s * s, 0, keepdims=True) + delta2
    one = jnp.ones((1, t.shape[1]), F32)
    lefts = [split3(-2.0 * s[k : k + 1] * weight) for k in range(3)]
    rights = [split3(t[k : k + 1]) for k in range(3)]
    lefts += [split3(square * weight), split3(weight)]
    rights += [(one,), split3(jnp.sum(t * t, 0, keepdims=True))]
    rows_l, rows_r = features(lefts, rights)
    left[...] = rows_l.T.astype(BF16)
    right[...] = rows_r.astype(BF16)

    @pl.loop(0, right.shape[1] // 256)
    def _(step):
        lanes = pl.ds(pl.multiple_of(step * 256, 256), 256)
        dist2 = jnp.dot(left[...], right[:, lanes], preferred_element_type=F32)
        block = lax.rsqrt(dist2).astype(BF16)
        tile[:, lanes] = block
        both = jnp.dot(split[...], block, preferred_element_type=F32)
        sums = both[:16] + both[16:]
        for i in range(4):
            out[step * 4 + i, :, :64] = sums[:, i * 64 : i * 64 + 64]
            out[step * 4 + i, :, 64:] = extra


def second_kernel(
    panels, recv, block, power_near, out, v_near, v_own, w_own, u_own, theta, factor, tmp
):
    total = tree_sum(recv)
    gram = total[:, 64:80]
    mean = total[0:1, 80:96] * (1.0 / panels)
    inverse = forward(gram, identity(gram.shape[0]))
    w = block[4:5, 64:] * block[:, :64] + total[:, :64]
    own = mm(inverse, jnp.concatenate([block[:, :64], w], 1))
    v, w = own[:, :64], own[:, 64:]
    u = w - mean[0:1, 0:1] * v
    tmp[:, :64] = u[:8]
    tmp[:, 64:] = u[8:]
    spread_out(out, tmp[...])
    theta[...] = mean
    factor[...] = mm(inverse, gram)
    v_near[...] = mm(inverse, power_near[...])
    v_own[...] = v
    w_own[...] = w
    u_own[...] = u


def third_kernel(recv, v_near, tile, out, u_split):
    u = jnp.concatenate([halves(recv, slice(0, 8), 0), halves(recv, slice(0, 8), 1)], 0)
    high = u.astype(BF16)
    u_split[0:16] = high
    u_split[16:32] = (u - high.astype(F32)).astype(BF16)
    extra = jnp.concatenate(
        [mm_t(v_near[...], u), mm_t(u, u), jnp.zeros((16, 32), F32)], 1
    )

    @pl.loop(0, tile.shape[1] // 256)
    def _(step):
        lanes = pl.ds(pl.multiple_of(step * 256, 256), 256)
        both = jnp.dot(u_split[...], tile[:, lanes], preferred_element_type=F32)
        sums = both[:16] + both[16:]
        for i in range(4):
            out[step * 4 + i, :, :64] = sums[:, i * 64 : i * 64 + 64]
            out[step * 4 + i, :, 64:] = extra


def fifth_kernel(
    recv, block, v_own, w_own, u_own, theta, factor, out, known, basis, images, tmp
):
    sums = tree_sum(recv)
    shifted = sums[:, 64:80]
    gram = sums[:, 80:96]
    v, w, u = v_own[...], w_own[...], u_own[...]
    x = block[4:5, 64:] * u + sums[:, :64]
    both = jnp.concatenate([x, u], 1) - t_mm(shifted, jnp.concatenate([w, v], 1))
    both = forward(gram - t_mm(shifted, shifted), both)
    small = mm_t(jnp.concatenate([w, both[:, :64], v], 0), both[:, :64])
    tmp[...] = jnp.zeros_like(tmp)
    for i in range(6):
        tmp[:, i * 16 : i * 16 + 16] = small[i * 8 : i * 8 + 8]
    spread_out(out, tmp[...])
    images[0:16] = w
    images[16:32] = both[:, :64]
    basis[0:16] = v
    basis[16:32] = both[:, 64:]
    shift = theta[0:1, 0:16] * identity(16)
    known[:, 0:16] = gram + theta[0:1, 0:16] * (shifted + shifted.T + shift)
    known[:, 16:32] = shifted.T + shift
    known[:, 32:48] = factor[...]


def sixth_kernel(recv, out):
    spread_out(out, tree_sum(recv))


def last_kernel(recv, known, basis, images, block, sol, res):
    total = tree_sum(recv)
    n12, n22, q2 = (
        jnp.concatenate([total[:, i : i + 16], total[:, i + 16 : i + 32]], 0)
        for i in (0, 32, 64)
    )
    system = jnp.concatenate(
        [
            jnp.concatenate([known[:, 0:16], n12, known[:, 16:32]], 1),
            jnp.concatenate([n12.T, n22, q2.T], 1),
        ],
        0,
    )
    coeff = mm(solve(system[:, :32], system[:, 32:]), known[:, 32:48])
    sol[...] = t_mm(coeff, basis[...])
    res[...] = block[:, :64] - t_mm(coeff, images[...])


def exchange(parts, axis, groups=None):
    return lax.all_to_all(parts, axis, 0, 0, axis_index_groups=groups)


def body(centroids, areas, conductance, power):
    nrhs, width = power.shape
    rows, cols = lax.axis_size("row"), lax.axis_size("col")
    panels = width * rows * cols
    scale = 4.0 / (math.pi * panels)
    delta2 = 16.0 / panels
    n_near, n_far = width * rows, width * cols
    own, square = ((nrhs, width), F32), ((nrhs, nrhs), F32)
    stack, fold = ((2 * nrhs, width), F32), [pltpu.VMEM((8, 128), F32)]
    twins = [(i, i ^ 1) for i in range(cols)]
    groups = [[r * cols + c for r in range(rows)] for c in range(0, cols, 2)]
    groups += [[r * cols + c for c in range(1, cols, 2)] for r in range(rows)]

    def place(x, row, lane):
        return jnp.pad(x, ((row, nrhs - row - x.shape[0]), (lane, 128 - lane - width)))

    block = (
        place(power, 0, 0)
        + place(centroids, 0, width)
        + place(areas[None, :], 3, width)
        + place(conductance[None, :], 4, width)
    )
    twin = lax.ppermute(block, "col", twins)
    (chunk,) = call(relay_kernel, [((rows, 2 * nrhs, 128), F32)], block, twin)
    recv = exchange(chunk, ("row", "col"), groups)
    (other,) = call(swap_kernel, [((rows, nrhs, 128), F32)], recv)
    got = lax.ppermute(other, "col", twins)
    parts, tile, power_near = call(
        functools.partial(first_kernel, scale, delta2),
        [((cols, 16, 128), F32), ((n_near, n_far), BF16), ((nrhs, n_near), F32)],
        recv, got,
        scratch=[
            pltpu.VMEM((n_near, 32), BF16),
            pltpu.VMEM((32, n_far), BF16),
            pltpu.VMEM((2 * nrhs, n_near), BF16),
        ],
    )
    recv = exchange(parts, "col")
    chunk, v_near, v_own, w_own, u_own, theta, factor = call(
        functools.partial(second_kernel, panels),
        [((rows, 8, 128), F32), ((nrhs, n_near), F32), own, own, own, ((1, nrhs), F32), square],
        recv, block, power_near,
        scratch=fold,
    )
    recv = exchange(chunk, "row")
    (parts,) = call(
        third_kernel, [((cols, 16, 128), F32)], recv, v_near, tile,
        scratch=[pltpu.VMEM((2 * nrhs, n_near), BF16)],
    )
    recv = exchange(parts, "col")
    chunk, known, basis, images = call(
        fifth_kernel, [((cols, 8, 128), F32), ((nrhs, 48), F32), stack, stack],
        recv, block, v_own, w_own, u_own, theta, factor,
        scratch=fold,
    )
    recv = exchange(chunk, "col")
    (chunk,) = call(sixth_kernel, [((rows, 8, 128), F32)], recv)
    recv = exchange(chunk, "row")
    return call(last_kernel, [own, own], recv, known, basis, images, block)


def solution(mesh):
    return jax.shard_map(
        body,
        mesh=mesh,
        in_specs=(
            P(None, ("col", "row")),
            P(("col", "row")),
            P(("col", "row")),
            P(None, ("col", "row")),
        ),
        out_specs=(P(None, ("col", "row")), P(None, ("col", "row"))),
        check_vma=False,
    )
```

```python
import functools
import math

import jax
import jax.numpy as jnp
from jax import lax
from jax.experimental import pallas as pl
from jax.experimental.pallas import tpu as pltpu
from jax.sharding import PartitionSpec as P

HIGH = lax.Precision.HIGHEST
F32 = jnp.float32
BF16 = jnp.bfloat16


def mm(a, b):
    return jnp.dot(a, b, precision=HIGH, preferred_element_type=F32)


def mm_t(a, b):
    return lax.dot_general(
        a, b, (((1,), (1,)), ((), ())), precision=HIGH, preferred_element_type=F32
    )


def t_mm(a, b):
    return lax.dot_general(
        a, b, (((0,), (0,)), ((), ())), precision=HIGH, preferred_element_type=F32
    )


def call(fn, outs, *args, scratch=()):
    vmem = pl.BlockSpec(memory_space=pltpu.VMEM)
    return pl.pallas_call(
        fn,
        out_shape=tuple(jax.ShapeDtypeStruct(shape, dtype) for shape, dtype in outs),
        in_specs=[pl.BlockSpec(memory_space=pltpu.VMEM)] * len(args),
        out_specs=tuple(vmem for _ in outs),
        scratch_shapes=list(scratch),
        compiler_params=pltpu.CompilerParams(vmem_limit_bytes=16 * 1024 * 1024),
    )(*args)


def block_pivots(a, n, below):
    row_id = lax.broadcasted_iota(jnp.int32, (n, 1), 0)
    for k in range(0, n, 2):
        row0, row1 = a[k : k + 1, :], a[k + 1 : k + 2, :]
        col0, col1 = a[:, k : k + 1], a[:, k + 1 : k + 2]
        p, q, r = row0[:, k : k + 1], row0[:, k + 1 : k + 2], row1[:, k + 1 : k + 2]
        det = p * r - q * q
        inv = 1.0 / det
        mix0, mix1 = r * row0 - q * row1, p * row1 - q * row0
        first, last = mix0 * inv, mix1 * inv
        new = a - col0 * first - col1 * last
        if below:
            first, last = row0 * lax.rsqrt(p), mix1 * lax.rsqrt(p * det)
            new = jnp.where(row_id > k, new, a)
        a = jnp.where(row_id == k, first, jnp.where(row_id == k + 1, last, new))
    return a[:, n:]


def forward(gram, right):
    return block_pivots(jnp.concatenate([gram, right], 1), gram.shape[0], True)


def identity(n):
    return (
        lax.broadcasted_iota(jnp.int32, (n, n), 0) == lax.broadcasted_iota(jnp.int32, (n, n), 1)
    ).astype(F32)


def solve(gram, right):
    return block_pivots(jnp.concatenate([gram, right], 1), gram.shape[0], False)


def spread_out(ref, chunk):
    for i in range(ref.shape[0]):
        ref[i] = chunk


def tree_sum(ref):
    parts = [ref[i] for i in range(ref.shape[0])]
    while len(parts) > 1:
        parts = [parts[i] + parts[i + 1] for i in range(0, len(parts), 2)]
    return parts[0]


def halves(ref, rows, side):
    lanes = slice(64 * side, 64 * side + 64)
    return jnp.concatenate([ref[i, rows, lanes] for i in range(ref.shape[0])], 1)


def split3(x):
    first = x.astype(BF16).astype(F32)
    second = (x - first).astype(BF16).astype(F32)
    return first, second, (x - first - second).astype(BF16).astype(F32)


def features(lefts, rights):
    out = [[], []]
    for left, right in zip(lefts, rights):
        for i, a in enumerate(left):
            for j, b in enumerate(right):
                if i + j < 3:
                    out[0].append(a)
                    out[1].append(b)
    n = len(out[0])
    for side in out:
        side.extend([jnp.zeros_like(side[0])] * (32 - n))
    return [jnp.concatenate(side, 0) for side in out]


def relay_kernel(block, twin, out):
    spread_out(out, jnp.concatenate([block[...], twin[...]], 1))


def is_odd():
    return lax.rem(lax.axis_index("col"), 2) == 1


def swap_kernel(recv, out):
    odd = is_odd()
    for i in range(out.shape[0]):
        places = recv[i, 16:24]
        out[i, 0:8, :64] = jnp.where(odd, places[:, :64], recv[i, 0:8, 64:])
        out[i, 0:8, 64:] = places[:, 64:]
        out[i, 8:16, :64] = recv[i, 8:16, 64:]
        out[i, 8:16, 64:] = places[:, 64:]


def first_kernel(scale, delta2, recv, got, out, tile, power_near, left, right, split):
    odd = is_odd()
    count = recv.shape[0]
    p = jnp.concatenate(
        [jnp.where(odd, got[i, :, :64], recv[i, 0:16, :64]) for i in range(count)], 1
    )
    src = jnp.concatenate(
        [jnp.where(odd, got[i, 0:8, 64:], recv[i, 16:24, :64]) for i in range(count)], 1
    )
    far = []
    for i in range(count):
        far.append(jnp.where(odd, recv[i, 16:24, 64:], got[i, 0:8, 64:]))
        far.append(jnp.where(odd, recv[i, 16:24, :64], got[i, 0:8, :64]))
    t = jnp.concatenate(far, 1)[0:3] - 0.5
    s = src[0:3, :] - 0.5
    inv = 1.0 / (src[3:4, :] * scale)
    weight = inv * inv
    square = jnp.sum(s * s, 0, keepdims=True) + delta2
    one = jnp.ones((1, t.shape[1]), F32)
    lefts = [split3(-2.0 * s[k : k + 1] * weight) for k in range(3)]
    rights = [split3(t[k : k + 1]) for k in range(3)]
    lefts += [split3(square * weight), split3(weight)]
    rights += [(one,), split3(jnp.sum(t * t, 0, keepdims=True))]
    rows_l, rows_r = features(lefts, rights)
    left[...] = rows_l.T.astype(BF16)
    right[...] = rows_r.astype(BF16)
    power_near[...] = p
    high = p.astype(BF16)
    split[0:16] = high
    split[16:32] = (p - high.astype(F32)).astype(BF16)
    mean = jnp.broadcast_to(jnp.sum(src[4:5, :], 1, keepdims=True), (16, 16))
    extra = jnp.concatenate([mm_t(p, p), mean, jnp.zeros((16, 32), F32)], 1)
    for step in range(right.shape[1] // 256):
        lanes = slice(step * 256, step * 256 + 256)
        dist2 = jnp.dot(left[...], right[:, lanes], preferred_element_type=F32)
        tile[:, lanes] = lax.rsqrt(dist2).astype(BF16)
    image(split, tile, extra, out)


def image(split, tile, extra, out):
    both = jnp.dot(split[...], tile[...], preferred_element_type=F32)
    sums = both[:16] + both[16:]
    for i in range(out.shape[0]):
        out[i, :, :64] = sums[:, i * 64 : i * 64 + 64]
        out[i, :, 64:] = extra


def second_kernel(
    panels, recv, block, power_near, out, v_near, v_own, w_own, u_own, theta, factor, tmp
):
    total = tree_sum(recv)
    gram = total[:, 64:80]
    mean = total[0:1, 80:96] * (1.0 / panels)
    inverse = forward(gram, identity(gram.shape[0]))
    w = block[20:21, :] * block[0:16, :] + total[:, :64]
    own = mm(inverse, jnp.concatenate([block[0:16, :], w], 1))
    v, w = own[:, :64], own[:, 64:]
    u = w - mean[0:1, 0:1] * v
    tmp[:, :64] = u[:8]
    tmp[:, 64:] = u[8:]
    spread_out(out, tmp[...])
    theta[...] = mean
    factor[...] = mm(inverse, gram)
    v_near[...] = mm(inverse, power_near[...])
    v_own[...] = v
    w_own[...] = w
    u_own[...] = u


def third_kernel(recv, v_near, tile, out, u_split):
    u = jnp.concatenate([halves(recv, slice(0, 8), 0), halves(recv, slice(0, 8), 1)], 0)
    high = u.astype(BF16)
    u_split[0:16] = high
    u_split[16:32] = (u - high.astype(F32)).astype(BF16)
    extra = jnp.concatenate(
        [mm_t(v_near[...], u), mm_t(u, u), jnp.zeros((16, 32), F32)], 1
    )
    image(u_split, tile, extra, out)


def fifth_kernel(
    recv, block, v_own, w_own, u_own, theta, factor, out, known, basis, images, tmp
):
    sums = tree_sum(recv)
    shifted = sums[:, 64:80]
    gram = sums[:, 80:96]
    v, w, u = v_own[...], w_own[...], u_own[...]
    x = block[20:21, :] * u + sums[:, :64]
    both = jnp.concatenate([x, u], 1) - t_mm(shifted, jnp.concatenate([w, v], 1))
    both = forward(gram - t_mm(shifted, shifted), both)
    small = mm_t(jnp.concatenate([w, both[:, :64], v], 0), both[:, :64])
    tmp[...] = jnp.zeros_like(tmp)
    for i in range(6):
        tmp[:, i * 16 : i * 16 + 16] = small[i * 8 : i * 8 + 8]
    spread_out(out, tmp[...])
    images[0:16] = w
    images[16:32] = both[:, :64]
    basis[0:16] = v
    basis[16:32] = both[:, 64:]
    shift = theta[0:1, 0:16] * identity(16)
    known[:, 0:16] = gram + theta[0:1, 0:16] * (shifted + shifted.T + shift)
    known[:, 16:32] = shifted.T + shift
    known[:, 32:48] = factor[...]


def sixth_kernel(recv, out):
    spread_out(out, tree_sum(recv))


def last_kernel(recv, known, basis, images, block, sol, res):
    total = tree_sum(recv)
    n12, n22, q2 = (
        jnp.concatenate([total[:, i : i + 16], total[:, i + 16 : i + 32]], 0)
        for i in (0, 32, 64)
    )
    system = jnp.concatenate(
        [
            jnp.concatenate([known[:, 0:16], n12, known[:, 16:32]], 1),
            jnp.concatenate([n12.T, n22, q2.T], 1),
        ],
        0,
    )
    coeff = mm(solve(system[:, :32], system[:, 32:]), known[:, 32:48])
    sol[...] = t_mm(coeff, basis[...])
    res[...] = block[0:16, :] - t_mm(coeff, images[...])


def exchange(parts, axis, groups=None):
    return lax.all_to_all(parts, axis, 0, 0, axis_index_groups=groups)


def body(centroids, areas, conductance, power):
    nrhs, width = power.shape
    rows, cols = lax.axis_size("row"), lax.axis_size("col")
    panels = width * rows * cols
    scale = 4.0 / (math.pi * panels)
    delta2 = 16.0 / panels
    n_near, n_far = width * rows, width * cols
    own, square = ((nrhs, width), F32), ((nrhs, nrhs), F32)
    stack, fold = ((2 * nrhs, width), F32), [pltpu.VMEM((8, 128), F32)]
    twins = [(i, i ^ 1) for i in range(cols)]
    groups = [[r * cols + c for r in range(rows)] for c in range(0, cols, 2)]
    groups += [[r * cols + c for c in range(1, cols, 2)] for r in range(rows)]

    def place(x, row):
        return jnp.pad(x, ((row, nrhs + 8 - row - x.shape[0]), (0, 0)))

    block = (
        place(power, 0)
        + place(centroids, nrhs)
        + place(areas[None, :], nrhs + 3)
        + place(conductance[None, :], nrhs + 4)
    )
    twin = lax.ppermute(block, "col", twins)
    (chunk,) = call(relay_kernel, [((rows, nrhs + 8, 128), F32)], block, twin)
    recv = exchange(chunk, ("row", "col"), groups)
    (other,) = call(swap_kernel, [((rows, nrhs, 128), F32)], recv)
    got = lax.ppermute(other, "col", twins)
    parts, tile, power_near = call(
        functools.partial(first_kernel, scale, delta2),
        [((cols, 16, 128), F32), ((n_near, n_far), BF16), ((nrhs, n_near), F32)],
        recv, got,
        scratch=[
            pltpu.VMEM((n_near, 32), BF16),
            pltpu.VMEM((32, n_far), BF16),
            pltpu.VMEM((2 * nrhs, n_near), BF16),
        ],
    )
    recv = exchange(parts, "col")
    chunk, v_near, v_own, w_own, u_own, theta, factor = call(
        functools.partial(second_kernel, panels),
        [((rows, 8, 128), F32), ((nrhs, n_near), F32), own, own, own, ((1, nrhs), F32), square],
        recv, block, power_near,
        scratch=fold,
    )
    recv = exchange(chunk, "row")
    (parts,) = call(
        third_kernel, [((cols, 16, 128), F32)], recv, v_near, tile,
        scratch=[pltpu.VMEM((2 * nrhs, n_near), BF16)],
    )
    recv = exchange(parts, "col")
    chunk, known, basis, images = call(
        fifth_kernel, [((cols, 8, 128), F32), ((nrhs, 48), F32), stack, stack],
        recv, block, v_own, w_own, u_own, theta, factor,
        scratch=fold,
    )
    recv = exchange(chunk, "col")
    (chunk,) = call(sixth_kernel, [((rows, 8, 128), F32)], recv)
    recv = exchange(chunk, "row")
    return call(last_kernel, [own, own], recv, known, basis, images, block)


def solution(mesh):
    return jax.shard_map(
        body,
        mesh=mesh,
        in_specs=(
            P(None, ("col", "row")),
            P(("col", "row")),
            P(("col", "row")),
            P(None, ("col", "row")),
        ),
        out_specs=(P(None, ("col", "row")), P(None, ("col", "row"))),
        check_vma=False,
    )
```

```python
import functools
import math

import jax
import jax.numpy as jnp
from jax import lax
from jax.experimental import pallas as pl
from jax.experimental.pallas import tpu as pltpu
from jax.sharding import PartitionSpec as P

HIGH = lax.Precision.HIGHEST
F32 = jnp.float32
BF16 = jnp.bfloat16


def mm(a, b):
    return jnp.dot(a, b, precision=HIGH, preferred_element_type=F32)


def mm_t(a, b):
    return lax.dot_general(
        a, b, (((1,), (1,)), ((), ())), precision=HIGH, preferred_element_type=F32
    )


def t_mm(a, b):
    return lax.dot_general(
        a, b, (((0,), (0,)), ((), ())), precision=HIGH, preferred_element_type=F32
    )


def call(fn, outs, *args, scratch=()):
    vmem = pl.BlockSpec(memory_space=pltpu.VMEM)
    return pl.pallas_call(
        fn,
        out_shape=tuple(jax.ShapeDtypeStruct(shape, dtype) for shape, dtype in outs),
        in_specs=[pl.BlockSpec(memory_space=pltpu.VMEM)] * len(args),
        out_specs=tuple(vmem for _ in outs),
        scratch_shapes=list(scratch),
        compiler_params=pltpu.CompilerParams(vmem_limit_bytes=16 * 1024 * 1024),
    )(*args)


def eliminate(gram, right, below):
    n = gram.shape[0]
    width = n + right.shape[1]
    count = -(-width // 128)
    parts = [gram, right]
    if count * 128 > width:
        parts.append(jnp.zeros((n, count * 128 - width), F32))
    a = jnp.concatenate(parts, 1)
    tiles = [a[:, i * 128 : i * 128 + 128] for i in range(count)]

    def full(x):
        return jnp.broadcast_to(x, (n, 128))

    row_id = lax.broadcasted_iota(jnp.int32, (n, 128), 0)
    scale = jnp.zeros((n, 128), F32)
    for start in range(0, n, 16):
        cols = [full(tiles[0][:, start + i : start + i + 1]) for i in range(16)]
        for i in range(16):
            k = start + i
            pivot = full(cols[i][k : k + 1, :])
            inv = 1.0 / pivot
            mask = row_id > k if below else row_id != k
            scale = jnp.where(row_id == k, lax.rsqrt(pivot) if below else inv, scale)
            factor = jnp.where(mask, cols[i], 0.0) * inv
            tiles = [t - factor * full(t[k : k + 1, :]) for t in tiles]
            cols = cols[: i + 1] + [c - factor * full(c[k : k + 1, :]) for c in cols[i + 1 :]]
    return jnp.concatenate([t * scale for t in tiles], 1)[:, n:width]


def identity(n):
    return (
        lax.broadcasted_iota(jnp.int32, (n, n), 0) == lax.broadcasted_iota(jnp.int32, (n, n), 1)
    ).astype(F32)


def spread_out(ref, chunk):
    for i in range(ref.shape[0]):
        ref[i] = chunk


def tree_sum(ref):
    parts = [ref[i] for i in range(ref.shape[0])]
    while len(parts) > 1:
        parts = [parts[i] + parts[i + 1] for i in range(0, len(parts), 2)]
    return parts[0]


def halves(ref, rows, side):
    lanes = slice(64 * side, 64 * side + 64)
    return jnp.concatenate([ref[i, rows, lanes] for i in range(ref.shape[0])], 1)


def split3(x):
    first = x.astype(BF16).astype(F32)
    second = (x - first).astype(BF16).astype(F32)
    return first, second, (x - first - second).astype(BF16).astype(F32)


def features(lefts, rights):
    out = [[], []]
    for left, right in zip(lefts, rights):
        for i, a in enumerate(left):
            for j, b in enumerate(right):
                if i + j < 3:
                    out[0].append(a)
                    out[1].append(b)
    n = len(out[0])
    for side in out:
        side.extend([jnp.zeros_like(side[0])] * (32 - n))
    return [jnp.concatenate(side, 0) for side in out]


def relay_kernel(block, twin, out):
    spread_out(out, jnp.concatenate([block[...], twin[...]], 1))


def is_odd():
    return lax.rem(lax.axis_index("col"), 2) == 1


def swap_kernel(recv, out):
    odd = is_odd()
    for i in range(out.shape[0]):
        places = recv[i, 16:24]
        out[i, 0:8, :64] = jnp.where(odd, places[:, :64], recv[i, 0:8, 64:])
        out[i, 0:8, 64:] = places[:, 64:]
        out[i, 8:16, :64] = recv[i, 8:16, 64:]
        out[i, 8:16, 64:] = places[:, 64:]


def first_kernel(scale, delta2, recv, got, out, tile, power_near, left, right, split):
    odd = is_odd()
    count = recv.shape[0]
    p = jnp.concatenate(
        [jnp.where(odd, got[i, :, :64], recv[i, 0:16, :64]) for i in range(count)], 1
    )
    src = jnp.concatenate(
        [jnp.where(odd, got[i, 0:8, 64:], recv[i, 16:24, :64]) for i in range(count)], 1
    )
    far = []
    for i in range(count):
        far.append(jnp.where(odd, recv[i, 16:24, 64:], got[i, 0:8, 64:]))
        far.append(jnp.where(odd, recv[i, 16:24, :64], got[i, 0:8, :64]))
    t = jnp.concatenate(far, 1)[0:3] - 0.5
    s = src[0:3, :] - 0.5
    inv = 1.0 / (src[3:4, :] * scale)
    weight = inv * inv
    square = jnp.sum(s * s, 0, keepdims=True) + delta2
    one = jnp.ones((1, t.shape[1]), F32)
    lefts = [split3(-2.0 * s[k : k + 1] * weight) for k in range(3)]
    rights = [split3(t[k : k + 1]) for k in range(3)]
    lefts += [split3(square * weight), split3(weight)]
    rights += [(one,), split3(jnp.sum(t * t, 0, keepdims=True))]
    rows_l, rows_r = features(lefts, rights)
    left[...] = rows_l.T.astype(BF16)
    right[...] = rows_r.astype(BF16)
    power_near[...] = p
    high = p.astype(BF16)
    split[0:16] = high
    split[16:32] = (p - high.astype(F32)).astype(BF16)
    mean = jnp.broadcast_to(jnp.sum(src[4:5, :], 1, keepdims=True), (16, 16))
    extra = jnp.concatenate([mm_t(p, p), mean, jnp.zeros((16, 32), F32)], 1)
    for step in range(right.shape[1] // 256):
        lanes = slice(step * 256, step * 256 + 256)
        dist2 = jnp.dot(left[...], right[:, lanes], preferred_element_type=F32)
        tile[:, lanes] = lax.rsqrt(dist2).astype(BF16)
    image(split, tile, extra, out)


def image(split, tile, extra, out):
    both = jnp.dot(split[...], tile[...], preferred_element_type=F32)
    sums = both[:16] + both[16:]
    for i in range(out.shape[0]):
        out[i, :, :64] = sums[:, i * 64 : i * 64 + 64]
        out[i, :, 64:] = extra


def second_kernel(
    panels, recv, block, power_near, out, v_near, v_own, w_own, u_own, theta, factor, tmp
):
    total = tree_sum(recv)
    gram = total[:, 64:80]
    mean = total[0:1, 80:96] * (1.0 / panels)
    p = block[0:16, :]
    u = (block[20:21, :] - mean[0:1, 0:1]) * p + total[:, :64]
    both = eliminate(gram, jnp.concatenate([identity(16), u], 1), True)
    inverse, u = both[:, :16], both[:, 16:]
    tmp[:, :64] = u[:8]
    tmp[:, 64:] = u[8:]
    spread_out(out, tmp[...])
    v = mm(inverse, p)
    theta[...] = mean
    factor[...] = mm(inverse, gram)
    v_near[...] = mm(inverse, power_near[...])
    v_own[...] = v
    w_own[...] = u + mean[0:1, 0:1] * v
    u_own[...] = u


def third_kernel(recv, v_near, tile, out, u_split):
    u = jnp.concatenate([halves(recv, slice(0, 8), 0), halves(recv, slice(0, 8), 1)], 0)
    high = u.astype(BF16)
    u_split[0:16] = high
    u_split[16:32] = (u - high.astype(F32)).astype(BF16)
    extra = jnp.concatenate(
        [mm_t(v_near[...], u), mm_t(u, u), jnp.zeros((16, 32), F32)], 1
    )
    image(u_split, tile, extra, out)


def fifth_kernel(
    recv, block, v_own, w_own, u_own, theta, factor, out, known, basis, images, tmp
):
    sums = tree_sum(recv)
    shifted = sums[:, 64:80]
    gram = sums[:, 80:96]
    v, w, u = v_own[...], w_own[...], u_own[...]
    x = block[20:21, :] * u + sums[:, :64]
    both = jnp.concatenate([x, u], 1) - t_mm(shifted, jnp.concatenate([w, v], 1))
    both = eliminate(gram - t_mm(shifted, shifted), both, True)
    small = mm_t(jnp.concatenate([w, both[:, :64], block[0:16, :]], 0), both[:, :64])
    tmp[...] = jnp.zeros_like(tmp)
    for i in range(6):
        tmp[:, i * 16 : i * 16 + 16] = small[i * 8 : i * 8 + 8]
    spread_out(out, tmp[...])
    images[0:16] = w
    images[16:32] = both[:, :64]
    basis[0:16] = v
    basis[16:32] = both[:, 64:]
    shift = theta[0:1, 0:16] * identity(16)
    known[:, 0:16] = gram + theta[0:1, 0:16] * (shifted + shifted.T + shift)
    known[:, 16:32] = mm(shifted.T + shift, factor[...])


def sixth_kernel(recv, out):
    spread_out(out, tree_sum(recv))


def last_kernel(recv, known, basis, images, block, sol, res):
    total = tree_sum(recv)
    n12, n22, q2 = (
        jnp.concatenate([total[:, i : i + 16], total[:, i + 16 : i + 32]], 0)
        for i in (0, 32, 64)
    )
    system = jnp.concatenate(
        [
            jnp.concatenate([known[:, 0:16], n12, known[:, 16:32]], 1),
            jnp.concatenate([n12.T, n22, q2.T], 1),
        ],
        0,
    )
    coeff = eliminate(system[:, :32], system[:, 32:], False)
    sol[...] = t_mm(coeff, basis[...])
    res[...] = block[0:16, :] - t_mm(coeff, images[...])


def exchange(parts, axis, groups=None):
    return lax.all_to_all(parts, axis, 0, 0, axis_index_groups=groups)


def body(centroids, areas, conductance, power):
    nrhs, width = power.shape
    rows, cols = lax.axis_size("row"), lax.axis_size("col")
    panels = width * rows * cols
    scale = 4.0 / (math.pi * panels)
    delta2 = 16.0 / panels
    n_near, n_far = width * rows, width * cols
    own, square = ((nrhs, width), F32), ((nrhs, nrhs), F32)
    stack, fold = ((2 * nrhs, width), F32), [pltpu.VMEM((8, 128), F32)]
    twins = [(i, i ^ 1) for i in range(cols)]
    groups = [[r * cols + c for r in range(rows)] for c in range(0, cols, 2)]
    groups += [[r * cols + c for c in range(1, cols, 2)] for r in range(rows)]

    def place(x, row):
        return jnp.pad(x, ((row, nrhs + 8 - row - x.shape[0]), (0, 0)))

    block = (
        place(power, 0)
        + place(centroids, nrhs)
        + place(areas[None, :], nrhs + 3)
        + place(conductance[None, :], nrhs + 4)
    )
    twin = lax.ppermute(block, "col", twins)
    (chunk,) = call(relay_kernel, [((rows, nrhs + 8, 128), F32)], block, twin)
    recv = exchange(chunk, ("row", "col"), groups)
    (other,) = call(swap_kernel, [((rows, nrhs, 128), F32)], recv)
    got = lax.ppermute(other, "col", twins)
    parts, tile, power_near = call(
        functools.partial(first_kernel, scale, delta2),
        [((cols, 16, 128), F32), ((n_near, n_far), BF16), ((nrhs, n_near), F32)],
        recv, got,
        scratch=[
            pltpu.VMEM((n_near, 32), BF16),
            pltpu.VMEM((32, n_far), BF16),
            pltpu.VMEM((2 * nrhs, n_near), BF16),
        ],
    )
    recv = exchange(parts, "col")
    chunk, v_near, v_own, w_own, u_own, theta, factor = call(
        functools.partial(second_kernel, panels),
        [((rows, 8, 128), F32), ((nrhs, n_near), F32), own, own, own, ((1, nrhs), F32), square],
        recv, block, power_near,
        scratch=fold,
    )
    recv = exchange(chunk, "row")
    (parts,) = call(
        third_kernel, [((cols, 16, 128), F32)], recv, v_near, tile,
        scratch=[pltpu.VMEM((2 * nrhs, n_near), BF16)],
    )
    recv = exchange(parts, "col")
    chunk, known, basis, images = call(
        fifth_kernel, [((cols, 8, 128), F32), ((nrhs, 2 * nrhs), F32), stack, stack],
        recv, block, v_own, w_own, u_own, theta, factor,
        scratch=fold,
    )
    recv = exchange(chunk, "col")
    (chunk,) = call(sixth_kernel, [((rows, 8, 128), F32)], recv)
    recv = exchange(chunk, "row")
    return call(last_kernel, [own, own], recv, known, basis, images, block)


def solution(mesh):
    return jax.shard_map(
        body,
        mesh=mesh,
        in_specs=(
            P(None, ("col", "row")),
            P(("col", "row")),
            P(("col", "row")),
            P(None, ("col", "row")),
        ),
        out_specs=(P(None, ("col", "row")), P(None, ("col", "row"))),
        check_vma=False,
    )
```

```python
import functools
import math

import jax
import jax.numpy as jnp
from jax import lax
from jax.experimental import pallas as pl
from jax.experimental.pallas import tpu as pltpu
from jax.sharding import PartitionSpec as P

HIGH = lax.Precision.HIGHEST
F32 = jnp.float32
BF16 = jnp.bfloat16


def mm(a, b):
    return jnp.dot(a, b, precision=HIGH, preferred_element_type=F32)


def mm_t(a, b):
    return lax.dot_general(
        a, b, (((1,), (1,)), ((), ())), precision=HIGH, preferred_element_type=F32
    )


def t_mm(a, b):
    return lax.dot_general(
        a, b, (((0,), (0,)), ((), ())), precision=HIGH, preferred_element_type=F32
    )


def call(fn, outs, *args, scratch=()):
    vmem = pl.BlockSpec(memory_space=pltpu.VMEM)
    return pl.pallas_call(
        fn,
        out_shape=tuple(jax.ShapeDtypeStruct(shape, dtype) for shape, dtype in outs),
        in_specs=[pl.BlockSpec(memory_space=pltpu.VMEM)] * len(args),
        out_specs=tuple(vmem for _ in outs),
        scratch_shapes=list(scratch),
        compiler_params=pltpu.CompilerParams(vmem_limit_bytes=16 * 1024 * 1024),
    )(*args)


def eliminate(gram, right, below):
    n = gram.shape[0]
    width = n + right.shape[1]
    count = -(-width // 128)
    parts = [gram, right]
    if count * 128 > width:
        parts.append(jnp.zeros((n, count * 128 - width), F32))
    a = jnp.concatenate(parts, 1)
    tiles = [a[:, i * 128 : i * 128 + 128] for i in range(count)]

    def full(x):
        return jnp.broadcast_to(x, (n, 128))

    row_id = lax.broadcasted_iota(jnp.int32, (n, 128), 0)
    scale = jnp.zeros((n, 128), F32)
    for start in range(0, n, 16):
        cols = [full(tiles[0][:, start + i : start + i + 1]) for i in range(16)]
        for i in range(16):
            k = start + i
            pivot = full(cols[i][k : k + 1, :])
            inv = 1.0 / pivot
            mask = row_id > k if below else row_id != k
            scale = jnp.where(row_id == k, lax.rsqrt(pivot) if below else inv, scale)
            factor = jnp.where(mask, cols[i], 0.0) * inv
            tiles = [t - factor * full(t[k : k + 1, :]) for t in tiles]
            cols = cols[: i + 1] + [c - factor * full(c[k : k + 1, :]) for c in cols[i + 1 :]]
    return jnp.concatenate([t * scale for t in tiles], 1)[:, n:width]


def identity(n):
    return (
        lax.broadcasted_iota(jnp.int32, (n, n), 0) == lax.broadcasted_iota(jnp.int32, (n, n), 1)
    ).astype(F32)


def spread_out(ref, chunk):
    for i in range(ref.shape[0]):
        ref[i] = chunk


def tree_sum(ref):
    parts = [ref[i] for i in range(ref.shape[0])]
    while len(parts) > 1:
        parts = [parts[i] + parts[i + 1] for i in range(0, len(parts), 2)]
    return parts[0]


def halves(ref, rows, side):
    lanes = slice(64 * side, 64 * side + 64)
    return jnp.concatenate([ref[i, rows, lanes] for i in range(ref.shape[0])], 1)


def split3(x):
    first = x.astype(BF16).astype(F32)
    second = (x - first).astype(BF16).astype(F32)
    return first, second, (x - first - second).astype(BF16).astype(F32)


def features(lefts, rights):
    out = [[], []]
    for left, right in zip(lefts, rights):
        for i, a in enumerate(left):
            for j, b in enumerate(right):
                if i + j < 3:
                    out[0].append(a)
                    out[1].append(b)
    n = len(out[0])
    for side in out:
        side.extend([jnp.zeros_like(side[0])] * (32 - n))
    return [jnp.concatenate(side, 0) for side in out]


def relay_kernel(block, twin, out):
    spread_out(out, jnp.concatenate([block[...], twin[...]], 1))


def is_odd():
    return lax.rem(lax.axis_index("col"), 2) == 1


def swap_kernel(recv, out):
    odd = is_odd()
    for i in range(out.shape[0]):
        places = recv[i, 16:24]
        out[i, 0:8, :64] = jnp.where(odd, places[:, :64], recv[i, 0:8, 64:])
        out[i, 0:8, 64:] = places[:, 64:]
        out[i, 8:16, :64] = recv[i, 8:16, 64:]
        out[i, 8:16, 64:] = places[:, 64:]


def first_kernel(scale, delta2, recv, got, out, tile, power_near, left, right, split):
    odd = is_odd()
    count = recv.shape[0]
    p = jnp.concatenate(
        [jnp.where(odd, got[i, :, :64], recv[i, 0:16, :64]) for i in range(count)], 1
    )
    src = jnp.concatenate(
        [jnp.where(odd, got[i, 0:8, 64:], recv[i, 16:24, :64]) for i in range(count)], 1
    )
    far = []
    for i in range(count):
        far.append(jnp.where(odd, recv[i, 16:24, 64:], got[i, 0:8, 64:]))
        far.append(jnp.where(odd, recv[i, 16:24, :64], got[i, 0:8, :64]))
    t = jnp.concatenate(far, 1)[0:3] - 0.5
    s = src[0:3, :] - 0.5
    inv = 1.0 / (src[3:4, :] * scale)
    weight = inv * inv
    square = jnp.sum(s * s, 0, keepdims=True) + delta2
    one = jnp.ones((1, t.shape[1]), F32)
    lefts = [split3(-2.0 * s[k : k + 1] * weight) for k in range(3)]
    rights = [split3(t[k : k + 1]) for k in range(3)]
    lefts += [split3(square * weight), split3(weight)]
    rights += [(one,), split3(jnp.sum(t * t, 0, keepdims=True))]
    rows_l, rows_r = features(lefts, rights)
    left[...] = rows_l.T.astype(BF16)
    right[...] = rows_r.astype(BF16)
    power_near[...] = p
    high = p.astype(BF16)
    split[0:16] = high
    split[16:32] = (p - high.astype(F32)).astype(BF16)
    mean = jnp.broadcast_to(jnp.sum(src[4:5, :], 1, keepdims=True), (4, 64))
    extra = jnp.concatenate(quarters(mm_t(p, p)) + [mean], 1)
    for step in range(right.shape[1] // 256):
        lanes = slice(step * 256, step * 256 + 256)
        dist2 = jnp.dot(left[...], right[:, lanes], preferred_element_type=F32)
        tile[:, lanes] = lax.rsqrt(dist2).astype(BF16)
    image(split, tile, extra, out)


def quarters(x):
    return [x[i : i + 4] for i in range(0, 16, 4)]


def image(split, tile, extra, out):
    both = jnp.dot(split[...], tile[...], preferred_element_type=F32)
    sums = both[:16] + both[16:]
    for i in range(out.shape[0]):
        part = quarters(sums[:, i * 64 : i * 64 + 64])
        for k in range(4):
            out[i, k // 2, :, 64 * (k % 2) : 64 * (k % 2) + 64] = part[k]
        out[i, 2] = extra


def collect(ref):
    total = tree_sum(ref)
    first, second, extra = total[0], total[1], total[2]
    parts = [first[:, :64], first[:, 64:], second[:, :64], second[:, 64:]]
    return jnp.concatenate(parts, 0), extra


def square_of(extra, lane):
    return jnp.concatenate([extra[:, lane + 16 * i : lane + 16 * i + 16] for i in range(4)], 0)


def second_kernel(
    panels, recv, block, power_near, out, v_near, v_own, w_own, u_own, theta, factor, tmp
):
    sums, extra = collect(recv)
    gram = square_of(extra, 0)
    mean = extra[0:1, 64:80] * (1.0 / panels)
    p = block[0:16, :]
    u = (block[20:21, :] - mean[0:1, 0:1]) * p + sums
    both = eliminate(gram, jnp.concatenate([identity(16), u], 1), True)
    inverse, u = both[:, :16], both[:, 16:]
    tmp[:, :64] = u[:8]
    tmp[:, 64:] = u[8:]
    spread_out(out, tmp[...])
    v = mm(inverse, p)
    theta[...] = mean
    factor[...] = mm(inverse, gram)
    v_near[...] = mm(inverse, power_near[...])
    v_own[...] = v
    w_own[...] = u + mean[0:1, 0:1] * v
    u_own[...] = u


def third_kernel(recv, v_near, tile, out, u_split):
    u = jnp.concatenate([halves(recv, slice(0, 8), 0), halves(recv, slice(0, 8), 1)], 0)
    high = u.astype(BF16)
    u_split[0:16] = high
    u_split[16:32] = (u - high.astype(F32)).astype(BF16)
    extra = jnp.concatenate(quarters(mm_t(v_near[...], u)) + quarters(mm_t(u, u)), 1)
    image(u_split, tile, extra, out)


def fifth_kernel(
    recv, block, v_own, w_own, u_own, theta, factor, out, known, basis, images, tmp
):
    sums, extra = collect(recv)
    shifted, gram = square_of(extra, 0), square_of(extra, 64)
    v, w, u = v_own[...], w_own[...], u_own[...]
    x = block[20:21, :] * u + sums
    both = jnp.concatenate([x, u], 1) - t_mm(shifted, jnp.concatenate([w, v], 1))
    both = eliminate(gram - t_mm(shifted, shifted), both, True)
    small = mm_t(jnp.concatenate([w, both[:, :64], block[0:16, :]], 0), both[:, :64])
    tmp[...] = jnp.zeros_like(tmp)
    for i in range(6):
        tmp[:, i * 16 : i * 16 + 16] = small[i * 8 : i * 8 + 8]
    spread_out(out, tmp[...])
    images[0:16] = w
    images[16:32] = both[:, :64]
    basis[0:16] = v
    basis[16:32] = both[:, 64:]
    shift = theta[0:1, 0:16] * identity(16)
    known[:, 0:16] = gram + theta[0:1, 0:16] * (shifted + shifted.T + shift)
    known[:, 16:32] = mm(shifted.T + shift, factor[...])


def sixth_kernel(recv, out):
    spread_out(out, tree_sum(recv))


def last_kernel(recv, known, basis, images, block, sol, res):
    total = tree_sum(recv)
    n12, n22, q2 = (
        jnp.concatenate([total[:, i : i + 16], total[:, i + 16 : i + 32]], 0)
        for i in (0, 32, 64)
    )
    system = jnp.concatenate(
        [
            jnp.concatenate([known[:, 0:16], n12, known[:, 16:32]], 1),
            jnp.concatenate([n12.T, n22, q2.T], 1),
        ],
        0,
    )
    coeff = eliminate(system[:, :32], system[:, 32:], False)
    sol[...] = t_mm(coeff, basis[...])
    res[...] = block[0:16, :] - t_mm(coeff, images[...])


def exchange(parts, axis, groups=None):
    return lax.all_to_all(parts, axis, 0, 0, axis_index_groups=groups)


def body(centroids, areas, conductance, power):
    nrhs, width = power.shape
    rows, cols = lax.axis_size("row"), lax.axis_size("col")
    panels = width * rows * cols
    scale = 4.0 / (math.pi * panels)
    delta2 = 16.0 / panels
    n_near, n_far = width * rows, width * cols
    own, square = ((nrhs, width), F32), ((nrhs, nrhs), F32)
    stack, fold = ((2 * nrhs, width), F32), [pltpu.VMEM((8, 128), F32)]
    twins = [(i, i ^ 1) for i in range(cols)]
    groups = [[r * cols + c for r in range(rows)] for c in range(0, cols, 2)]
    groups += [[r * cols + c for c in range(1, cols, 2)] for r in range(rows)]

    def place(x, row):
        return jnp.pad(x, ((row, nrhs + 8 - row - x.shape[0]), (0, 0)))

    block = (
        place(power, 0)
        + place(centroids, nrhs)
        + place(areas[None, :], nrhs + 3)
        + place(conductance[None, :], nrhs + 4)
    )
    twin = lax.ppermute(block, "col", twins)
    (chunk,) = call(relay_kernel, [((rows, nrhs + 8, 128), F32)], block, twin)
    recv = exchange(chunk, ("row", "col"), groups)
    (other,) = call(swap_kernel, [((rows, nrhs, 128), F32)], recv)
    got = lax.ppermute(other, "col", twins)
    parts, tile, power_near = call(
        functools.partial(first_kernel, scale, delta2),
        [((cols, 3, 4, 128), F32), ((n_near, n_far), BF16), ((nrhs, n_near), F32)],
        recv, got,
        scratch=[
            pltpu.VMEM((n_near, 32), BF16),
            pltpu.VMEM((32, n_far), BF16),
            pltpu.VMEM((2 * nrhs, n_near), BF16),
        ],
    )
    recv = exchange(parts, "col")
    chunk, v_near, v_own, w_own, u_own, theta, factor = call(
        functools.partial(second_kernel, panels),
        [((rows, 8, 128), F32), ((nrhs, n_near), F32), own, own, own, ((1, nrhs), F32), square],
        recv, block, power_near,
        scratch=fold,
    )
    recv = exchange(chunk, "row")
    (parts,) = call(
        third_kernel, [((cols, 3, 4, 128), F32)], recv, v_near, tile,
        scratch=[pltpu.VMEM((2 * nrhs, n_near), BF16)],
    )
    recv = exchange(parts, "col")
    chunk, known, basis, images = call(
        fifth_kernel, [((cols, 8, 128), F32), ((nrhs, 2 * nrhs), F32), stack, stack],
        recv, block, v_own, w_own, u_own, theta, factor,
        scratch=fold,
    )
    recv = exchange(chunk, "col")
    (chunk,) = call(sixth_kernel, [((rows, 8, 128), F32)], recv)
    recv = exchange(chunk, "row")
    return call(last_kernel, [own, own], recv, known, basis, images, block)


def solution(mesh):
    return jax.shard_map(
        body,
        mesh=mesh,
        in_specs=(
            P(None, ("col", "row")),
            P(("col", "row")),
            P(("col", "row")),
            P(None, ("col", "row")),
        ),
        out_specs=(P(None, ("col", "row")), P(None, ("col", "row"))),
        check_vma=False,
    )
```

```python
import functools
import math

import jax
import jax.numpy as jnp
from jax import lax
from jax.experimental import pallas as pl
from jax.experimental.pallas import tpu as pltpu
from jax.sharding import PartitionSpec as P

HIGH = lax.Precision.HIGHEST
F32 = jnp.float32
BF16 = jnp.bfloat16


def mm(a, b):
    return jnp.dot(a, b, precision=HIGH, preferred_element_type=F32)


def mm_t(a, b):
    return lax.dot_general(
        a, b, (((1,), (1,)), ((), ())), precision=HIGH, preferred_element_type=F32
    )


def t_mm(a, b):
    return lax.dot_general(
        a, b, (((0,), (0,)), ((), ())), precision=HIGH, preferred_element_type=F32
    )


def call(fn, outs, *args, scratch=()):
    vmem = pl.BlockSpec(memory_space=pltpu.VMEM)
    return pl.pallas_call(
        fn,
        out_shape=tuple(jax.ShapeDtypeStruct(shape, dtype) for shape, dtype in outs),
        in_specs=[pl.BlockSpec(memory_space=pltpu.VMEM)] * len(args),
        out_specs=tuple(vmem for _ in outs),
        scratch_shapes=list(scratch),
        compiler_params=pltpu.CompilerParams(vmem_limit_bytes=16 * 1024 * 1024),
    )(*args)


def eliminate(gram, right, below):
    n = gram.shape[0]
    width = n + right.shape[1]
    count = -(-width // 128)
    parts = [gram, right]
    if count * 128 > width:
        parts.append(jnp.zeros((n, count * 128 - width), F32))
    a = jnp.concatenate(parts, 1)
    tiles = [a[:, i * 128 : i * 128 + 128] for i in range(count)]

    def full(x):
        return jnp.broadcast_to(x, (n, 128))

    row_id = lax.broadcasted_iota(jnp.int32, (n, 128), 0)
    scale = jnp.zeros((n, 128), F32)
    for start in range(0, n, 16):
        cols = [full(tiles[0][:, start + i : start + i + 1]) for i in range(16)]
        for i in range(16):
            k = start + i
            pivot = full(cols[i][k : k + 1, :])
            inv = 1.0 / pivot
            mask = row_id > k if below else row_id != k
            scale = jnp.where(row_id == k, lax.rsqrt(pivot) if below else inv, scale)
            factor = jnp.where(mask, cols[i], 0.0) * inv
            tiles = [t - factor * full(t[k : k + 1, :]) for t in tiles]
            cols = cols[: i + 1] + [c - factor * full(c[k : k + 1, :]) for c in cols[i + 1 :]]
    return jnp.concatenate([t * scale for t in tiles], 1)[:, n:width]


def identity(n):
    return (
        lax.broadcasted_iota(jnp.int32, (n, n), 0) == lax.broadcasted_iota(jnp.int32, (n, n), 1)
    ).astype(F32)


def spread_out(ref, chunk):
    for i in range(ref.shape[0]):
        ref[i] = chunk


def tree_sum(ref):
    parts = [ref[i] for i in range(ref.shape[0])]
    while len(parts) > 1:
        parts = [parts[i] + parts[i + 1] for i in range(0, len(parts), 2)]
    return parts[0]


def halves(ref, rows, side):
    lanes = slice(64 * side, 64 * side + 64)
    return jnp.concatenate([ref[i, rows, lanes] for i in range(ref.shape[0])], 1)


def split3(x):
    first = x.astype(BF16).astype(F32)
    second = (x - first).astype(BF16).astype(F32)
    return first, second, (x - first - second).astype(BF16).astype(F32)


def features(lefts, rights):
    out = [[], []]
    for left, right in zip(lefts, rights):
        for i, a in enumerate(left):
            for j, b in enumerate(right):
                if i + j < 3:
                    out[0].append(a)
                    out[1].append(b)
    n = len(out[0])
    for side in out:
        side.extend([jnp.zeros_like(side[0])] * (32 - n))
    return [jnp.concatenate(side, 0) for side in out]


def relay_kernel(block, twin, out):
    spread_out(out, jnp.concatenate([block[...], twin[...]], 1))


def is_odd():
    return lax.rem(lax.axis_index("col"), 2) == 1


def swap_kernel(recv, out):
    odd = is_odd()
    for i in range(out.shape[0]):
        places = recv[i, 16:24]
        out[i, 0:8, :64] = jnp.where(odd, places[:, :64], recv[i, 0:8, 64:])
        out[i, 0:8, 64:] = places[:, 64:]
        out[i, 8:16, :64] = recv[i, 8:16, 64:]
        out[i, 8:16, 64:] = places[:, 64:]


def first_kernel(scale, delta2, recv, got, out, tile, power_near, left, right, split):
    odd = is_odd()
    count = recv.shape[0]
    p = jnp.concatenate(
        [jnp.where(odd, got[i, :, :64], recv[i, 0:16, :64]) for i in range(count)], 1
    )
    src = jnp.concatenate(
        [jnp.where(odd, got[i, 0:8, 64:], recv[i, 16:24, :64]) for i in range(count)], 1
    )
    far = []
    for i in range(count):
        far.append(jnp.where(odd, recv[i, 16:24, 64:], got[i, 0:8, 64:]))
        far.append(jnp.where(odd, recv[i, 16:24, :64], got[i, 0:8, :64]))
    t = jnp.concatenate(far, 1)[0:3] - 0.5
    s = src[0:3, :] - 0.5
    inv = 1.0 / (src[3:4, :] * scale)
    weight = inv * inv
    square = jnp.sum(s * s, 0, keepdims=True) + delta2
    one = jnp.ones((1, t.shape[1]), F32)
    lefts = [split3(-2.0 * s[k : k + 1] * weight) for k in range(3)]
    rights = [split3(t[k : k + 1]) for k in range(3)]
    lefts += [split3(square * weight), split3(weight)]
    rights += [(one,), split3(jnp.sum(t * t, 0, keepdims=True))]
    rows_l, rows_r = features(lefts, rights)
    left[...] = rows_l.T.astype(BF16)
    right[...] = rows_r.astype(BF16)
    power_near[...] = p
    high = p.astype(BF16)
    split[0:16] = high
    split[16:32] = (p - high.astype(F32)).astype(BF16)
    mean = jnp.broadcast_to(jnp.sum(src[4:5, :], 1, keepdims=True), (4, 64))
    extra = jnp.concatenate(quarters(mm_t(p, p)) + [mean], 1)
    for step in range(right.shape[1] // 256):
        lanes = slice(step * 256, step * 256 + 256)
        dist2 = jnp.dot(left[...], right[:, lanes], preferred_element_type=F32)
        tile[:, lanes] = lax.rsqrt(dist2).astype(BF16)
    image(split, tile, extra, out)


def quarters(x):
    return [x[i : i + 4] for i in range(0, 16, 4)]


def image(split, tile, extra, out):
    both = jnp.dot(split[...], tile[...], preferred_element_type=F32)
    sums = both[:16] + both[16:]
    for i in range(out.shape[0]):
        part = quarters(sums[:, i * 64 : i * 64 + 64])
        for k in range(4):
            out[i, k // 2, :, 64 * (k % 2) : 64 * (k % 2) + 64] = part[k]
        out[i, 2] = extra


def collect(ref):
    total = tree_sum(ref)
    first, second, extra = total[0], total[1], total[2]
    parts = [first[:, :64], first[:, 64:], second[:, :64], second[:, 64:]]
    return jnp.concatenate(parts, 0), extra


def square_of(extra, lane):
    return jnp.concatenate([extra[:, lane + 16 * i : lane + 16 * i + 16] for i in range(4)], 0)


def second_kernel(
    panels, recv, block, power_near, out, v_near, v_own, w_own, u_own, theta, factor, tmp
):
    sums, extra = collect(recv)
    gram = square_of(extra, 0)
    mean = extra[0:1, 64:80] * (1.0 / panels)
    p = block[0:16, :]
    u = (block[20:21, :] - mean[0:1, 0:1]) * p + sums
    both = eliminate(gram, jnp.concatenate([identity(16), u], 1), True)
    inverse, u = both[:, :16], both[:, 16:]
    tmp[:, :64] = u[:8]
    tmp[:, 64:] = u[8:]
    spread_out(out, tmp[...])
    v = mm(inverse, p)
    theta[...] = mean
    factor[...] = mm(inverse, gram)
    v_near[...] = mm(inverse, power_near[...])
    v_own[...] = v
    w_own[...] = u + mean[0:1, 0:1] * v
    u_own[...] = u


def third_kernel(recv, v_near, tile, out, u_split):
    u = jnp.concatenate([halves(recv, slice(0, 8), 0), halves(recv, slice(0, 8), 1)], 0)
    high = u.astype(BF16)
    u_split[0:16] = high
    u_split[16:32] = (u - high.astype(F32)).astype(BF16)
    extra = jnp.concatenate(quarters(mm_t(v_near[...], u)) + quarters(mm_t(u, u)), 1)
    image(u_split, tile, extra, out)


def fifth_kernel(
    recv, block, v_own, w_own, u_own, theta, factor, out, known, basis, images, tmp
):
    sums, extra = collect(recv)
    shifted, gram = square_of(extra, 0), square_of(extra, 64)
    v, w, u = v_own[...], w_own[...], u_own[...]
    x = block[20:21, :] * u + sums
    both = jnp.concatenate([x, u], 1) - t_mm(shifted, jnp.concatenate([w, v], 1))
    both = eliminate(gram - t_mm(shifted, shifted), both, True)
    image2 = both[:, :64]
    lower = mm_t(image2, jnp.concatenate([w, image2, block[0:16, :]], 0))
    upper = mm_t(w, image2)
    tmp[:, 0:48] = lower[:8]
    tmp[:, 48:96] = lower[8:]
    tmp[:, 96:112] = upper[:8]
    tmp[:, 112:128] = upper[8:]
    spread_out(out, tmp[...])
    images[0:16] = w
    images[16:32] = both[:, :64]
    basis[0:16] = v
    basis[16:32] = both[:, 64:]
    shift = theta[0:1, 0:16] * identity(16)
    known[:, 0:16] = gram + theta[0:1, 0:16] * (shifted + shifted.T + shift)
    known[:, 16:32] = mm(shifted.T + shift, factor[...])


def sixth_kernel(recv, out):
    spread_out(out, tree_sum(recv))


def last_kernel(recv, known, basis, images, block, sol, res):
    total = tree_sum(recv)
    n12 = jnp.concatenate([total[:, 96:112], total[:, 112:128]], 0)
    system = jnp.concatenate(
        [
            jnp.concatenate([known[:, 0:16], n12, known[:, 16:32]], 1),
            total[:, 0:48],
            total[:, 48:96],
        ],
        0,
    )
    coeff = eliminate(system[:, :32], system[:, 32:], False)
    sol[...] = t_mm(coeff, basis[...])
    res[...] = block[0:16, :] - t_mm(coeff, images[...])


def exchange(parts, axis, groups=None):
    return lax.all_to_all(parts, axis, 0, 0, axis_index_groups=groups)


def body(centroids, areas, conductance, power):
    nrhs, width = power.shape
    rows, cols = lax.axis_size("row"), lax.axis_size("col")
    panels = width * rows * cols
    scale = 4.0 / (math.pi * panels)
    delta2 = 16.0 / panels
    n_near, n_far = width * rows, width * cols
    own, square = ((nrhs, width), F32), ((nrhs, nrhs), F32)
    stack, fold = ((2 * nrhs, width), F32), [pltpu.VMEM((8, 128), F32)]
    twins = [(i, i ^ 1) for i in range(cols)]
    groups = [[r * cols + c for r in range(rows)] for c in range(0, cols, 2)]
    groups += [[r * cols + c for c in range(1, cols, 2)] for r in range(rows)]

    def place(x, row):
        return jnp.pad(x, ((row, nrhs + 8 - row - x.shape[0]), (0, 0)))

    block = (
        place(power, 0)
        + place(centroids, nrhs)
        + place(areas[None, :], nrhs + 3)
        + place(conductance[None, :], nrhs + 4)
    )
    twin = lax.ppermute(block, "col", twins)
    (chunk,) = call(relay_kernel, [((rows, nrhs + 8, 128), F32)], block, twin)
    recv = exchange(chunk, ("row", "col"), groups)
    (other,) = call(swap_kernel, [((rows, nrhs, 128), F32)], recv)
    got = lax.ppermute(other, "col", twins)
    parts, tile, power_near = call(
        functools.partial(first_kernel, scale, delta2),
        [((cols, 3, 4, 128), F32), ((n_near, n_far), BF16), ((nrhs, n_near), F32)],
        recv, got,
        scratch=[
            pltpu.VMEM((n_near, 32), BF16),
            pltpu.VMEM((32, n_far), BF16),
            pltpu.VMEM((2 * nrhs, n_near), BF16),
        ],
    )
    recv = exchange(parts, "col")
    chunk, v_near, v_own, w_own, u_own, theta, factor = call(
        functools.partial(second_kernel, panels),
        [((rows, 8, 128), F32), ((nrhs, n_near), F32), own, own, own, ((1, nrhs), F32), square],
        recv, block, power_near,
        scratch=fold,
    )
    recv = exchange(chunk, "row")
    (parts,) = call(
        third_kernel, [((cols, 3, 4, 128), F32)], recv, v_near, tile,
        scratch=[pltpu.VMEM((2 * nrhs, n_near), BF16)],
    )
    recv = exchange(parts, "col")
    chunk, known, basis, images = call(
        fifth_kernel, [((cols, 8, 128), F32), ((nrhs, 2 * nrhs), F32), stack, stack],
        recv, block, v_own, w_own, u_own, theta, factor,
        scratch=fold,
    )
    recv = exchange(chunk, "col")
    (chunk,) = call(sixth_kernel, [((rows, 8, 128), F32)], recv)
    recv = exchange(chunk, "row")
    return call(last_kernel, [own, own], recv, known, basis, images, block)


def solution(mesh):
    return jax.shard_map(
        body,
        mesh=mesh,
        in_specs=(
            P(None, ("col", "row")),
            P(("col", "row")),
            P(("col", "row")),
            P(None, ("col", "row")),
        ),
        out_specs=(P(None, ("col", "row")), P(None, ("col", "row"))),
        check_vma=False,
    )
```
